32 devices in a mesh: groups: 2 (over x), dom: 16 (over z, y, core).
Axes of the slice: x: 2, y: 2, z: 4, core: 2. Of those that a mesh axis runs over, the one named last changes fastest.
Arguments:
- features: bfloat16 [8192, 256], P(('groups', 'dom')), parts along dimension 0, may hold values from -6 to 6
- out_grad: bfloat16 [8192, 256], P(('groups', 'dom')), parts along dimension 0, may hold values from -6 to 6
- send_weight: bfloat16 [256, 256], replicated, may hold values from -0.375 to 0.375
- recv_weight: bfloat16 [256, 256], replicated, may hold values from -0.375 to 0.375
- edge_bias: float32 [256], replicated, may hold values from -1 to 1
- coarse_weight: bfloat16 [256, 256], replicated, may hold values from -0.375 to 0.375
- top_weight: float32 [256, 256], replicated, may hold values from -0.375 to 0.375
- out_weight: bfloat16 [256, 256], replicated, may hold values from -0.375 to 0.375
- edge_sender: int32 [32, 2048], P(('groups', 'dom')), parts along dimension 0, may hold values from 0 to 383
- edge_receiver: int32 [32, 2048], P(('groups', 'dom')), parts along dimension 0, may hold values from 0 to 255
- halo_rows: int32 [32, 4, 32], P(('groups', 'dom')), parts along dimension 0, may hold values from 0 to 255
- owner_slot: int32 [32, 256], P(('groups', 'dom')), parts along dimension 0, may hold values from 0 to 639, as said below
- cluster_index: int32 [32, 256], P(('groups', 'dom')), parts along dimension 0, may hold values from 0 to 15
- slot_coarse: int32 [32, 640], P(('groups', 'dom')), parts along dimension 0, may hold values from 0 to 16, as said below
- coarse_parent: int32 [512], P(('groups', 'dom')), parts along dimension 0, may hold values from 0 to 255
Outputs:
- updated: bfloat16 [8192, 256], P(('groups', 'dom')), parts along dimension 0
- feature_grad: float32 [8192, 256], P(('groups', 'dom')), parts along dimension 0
- send_weight_grad: float32 [512, 256], P('groups'), parts along dimension 0
- recv_weight_grad: float32 [512, 256], P('groups'), parts along dimension 0
- edge_bias_grad: float32 [512], P('groups'), parts along dimension 0
- coarse_weight_grad: float32 [512, 256], P('groups'), parts along dimension 0
- top_weight_grad: float32 [512, 256], P('groups'), parts along dimension 0
- out_weight_grad: float32 [512, 256], P('groups'), parts along dimension 0
The draws below stay inside these ranges and needn't reach their ends.
There are 2 independent parts, one for each index of `groups`. The reference program is written for one: setup_inputs(seed, part) draws one part's arguments, and reference() takes and returns one part's arrays. A program takes and returns all parts, laid end to end along the dimension named above; an argument that names none is the same for every part. Nothing has to cross between parts.
Inputs may be any that keep to these rules, and one draw needn't show every extreme that they name: Within one partition all places differ; the owner of a row is owner_slot // 40; in every draw one owner takes all 40 places of every partition. slot_coarse[o, p * 40 + j] equals cluster_index of the row of partition p whose owner_slot is o * 40 + j, and 16 where no row has that place.
All inputs are finite; a program needn't handle non-finite values.
Results may differ from the reference program's by a relative error of at most 0.0073.
Values may be sent and summed in bfloat16 or wider, within the bound.
A program may use at most 64 MiB of HBM per device.

```python
import jax
import jax.numpy as jnp
from jax import lax

H = 256
NF_DEV = 256
DEG = 8
PW = 8
NCC = 256
DOMAINS = 16
NF = 4096
NC_DEV = 16
NC = 256
SLOTS = 32
EF_DEV = 2048
CAP = 40


def routing(key):
    slot_count = DOMAINS * CAP
    key_busy, key_noise, key_order, key_local = jax.random.split(key, 4)
    busy_owner = jax.random.randint(key_busy, (), 0, DOMAINS)
    noise_bits = jax.random.randint(key_noise, (DOMAINS, slot_count), 0, 1024)
    position = jnp.arange(slot_count, dtype=jnp.int32)
    boost = jnp.where(position // CAP == busy_owner, 1 << 26, 0)
    priority = noise_bits * slot_count + position[None, :] + boost[None, :]
    chosen = lax.top_k(priority, NF_DEV)[1].astype(jnp.int32)
    orders = jax.vmap(lambda part_key: jax.random.permutation(part_key, NF_DEV))(jax.random.split(key_order, DOMAINS))
    owner_slot = jnp.take_along_axis(chosen, orders.astype(jnp.int32), axis=1)
    part_ids = jnp.arange(DOMAINS, dtype=jnp.int32)
    live_slots = jnp.zeros((DOMAINS, slot_count), jnp.int32).at[part_ids[:, None], chosen].set(1)
    local_ids = jax.random.randint(key_local, (DOMAINS, DOMAINS, CAP), 0, NC_DEV)
    live_view = live_slots.reshape(DOMAINS, DOMAINS, CAP).transpose(1, 0, 2)
    slot_coarse = jnp.where(live_view == 1, local_ids, NC_DEV).reshape(DOMAINS, slot_count)
    cluster_index = local_ids[owner_slot // CAP, part_ids[:, None], owner_slot % CAP]
    return (owner_slot, cluster_index, slot_coarse)


def draw_owner_slot(key, part):
    shared = routing(key)
    return shared[0]


def draw_cluster_index(key, part):
    shared = routing(key)
    return shared[1]


def draw_slot_coarse(key, part):
    shared = routing(key)
    return shared[2]


def place_ends(array, rng, low, top_value):
    place = [jax.random.randint(jax.random.fold_in(rng, axis), (), 0, length) for axis, length in enumerate(array.shape)]
    main_axis = array.shape.index(max(array.shape))
    beside = place[:main_axis] + [(place[main_axis] + 1) % array.shape[main_axis]] + place[main_axis + 1:]
    return array.at[tuple(place)].set(low).at[tuple(beside)].set(top_value)


def steps_of(stream_key, dims, pieces, least, largest):
    factor_of, own = 1.0, jax.random.fold_in(stream_key, 6)
    for dim, parts in pieces:
        draws = jnp.exp(jax.random.uniform(jax.random.fold_in(own, dim), (parts,), jnp.float32, least / len(pieces), largest / len(pieces)))
        factor_of = factor_of * jnp.repeat(draws, dims[dim] // parts).reshape([-1 if axis == dim else 1 for axis in range(len(dims))])
    return factor_of


def gaussian(rng, extent, deviation, most, cuts=(), kind=jnp.bfloat16):
    array = jax.random.normal(rng, extent, jnp.float32) * deviation
    if len(cuts) > 0:
        array = steps_of(rng, extent, cuts, -0.22, 0.18) * array
    return jnp.clip(array, min=-most, max=most).astype(kind)


def setup_inputs(seed: int = 0, part: int = 0) -> dict:
    seeds = jax.random.split(jax.random.key(seed), 16)
    own_keys = jax.random.split(jax.random.fold_in(seeds[15], part), 16)
    return {
        "features": gaussian(own_keys[0], (NF, H), 1.0, 6.0, ((0, 16),)),
        "out_grad": gaussian(own_keys[1], (NF, H), 1.0, 6.0, ((0, 16),)),
        "send_weight": gaussian(seeds[2], (H, H), H ** -0.5, 0.375),
        "recv_weight": gaussian(seeds[3], (H, H), H ** -0.5, 0.375),
        "edge_bias": jnp.clip(jax.random.uniform(seeds[4], (H,), jnp.float32, -1.0, 1.0), -1.0, 1.0),
        "coarse_weight": gaussian(seeds[5], (H, H), H ** -0.5, 0.375),
        "top_weight": gaussian(seeds[6], (H, H), H ** -0.5, 0.375, (), jnp.float32),
        "out_weight": gaussian(seeds[7], (H, H), H ** -0.5, 0.375),
        "edge_sender": place_ends(jax.random.randint(own_keys[8], (DOMAINS, EF_DEV), 0, NF_DEV + 4 * SLOTS), jax.random.fold_in(own_keys[8], 1), 0, (NF_DEV + 4 * SLOTS) - 1).astype(jnp.int32),
        "edge_receiver": place_ends(jax.random.randint(own_keys[9], (DOMAINS, EF_DEV), 0, NF_DEV), jax.random.fold_in(own_keys[9], 1), 0, NF_DEV - 1).astype(jnp.int32),
        "halo_rows": place_ends(jax.random.randint(own_keys[10], (DOMAINS, 4, SLOTS), 0, NF_DEV), jax.random.fold_in(own_keys[10], 1), 0, NF_DEV - 1).astype(jnp.int32),
        "owner_slot": draw_owner_slot(jax.random.fold_in(jax.random.fold_in(seeds[15], part), 71), part),
        "cluster_index": draw_cluster_index(jax.random.fold_in(jax.random.fold_in(seeds[15], part), 71), part),
        "slot_coarse": draw_slot_coarse(jax.random.fold_in(jax.random.fold_in(seeds[15], part), 71), part),
        "coarse_parent": place_ends(jax.random.randint(own_keys[14], (NC,), 0, NCC), jax.random.fold_in(own_keys[14], 1), 0, NCC - 1).astype(jnp.int32),
    }


def silu_grad(values):
    gate = jax.nn.sigmoid(values)
    return gate * (1.0 + values * (1.0 - gate))

def offset_list():
    return (1, -1, PW, -PW)

def halo_table(by_part, halo_rows):
    part_ids = jnp.arange(DOMAINS, dtype=jnp.int32)
    blocks = []
    for direction, offset in enumerate(offset_list()):
        source = part_ids - offset
        present = (source >= 0) & (source < DOMAINS)
        clipped = jnp.clip(source, 0, DOMAINS - 1)
        row_ids = halo_rows[clipped, direction]
        fetched = by_part[clipped[:, None], row_ids]
        blocks.append(jnp.where(present[:, None, None], fetched, jnp.zeros_like(fetched)))
    return jnp.concatenate(blocks, axis=1)

def restrict(row_parts, owner_slot, slot_coarse):
    feature_width = row_parts.shape[2]

    def fill_slots(operands):
        row_values, slot_list = operands
        return jnp.zeros((DOMAINS * CAP, feature_width), row_values.dtype).at[slot_list].set(row_values)
    buffers = lax.map(fill_slots, (row_parts, owner_slot))
    arrived = buffers.reshape(DOMAINS, DOMAINS, CAP, feature_width).transpose(1, 0, 2, 3)
    arrived = arrived.reshape(DOMAINS, DOMAINS * CAP, feature_width)

    def collect_rows(operands):
        fetched, slot_ids = operands
        summed = jax.ops.segment_sum(fetched.astype(jnp.float32), slot_ids, num_segments=NC_DEV + 1)
        return summed[:NC_DEV]
    return lax.map(collect_rows, (arrived, slot_coarse)).reshape(DOMAINS * NC_DEV, feature_width)

def reference(features, out_grad, send_weight, recv_weight, edge_bias, coarse_weight, top_weight, out_weight, edge_sender, edge_receiver, halo_rows, owner_slot, cluster_index, slot_coarse, coarse_parent):
    feature_width = features.shape[1]
    highest = lax.Precision.HIGHEST
    by_part = features.reshape(DOMAINS, NF_DEV, feature_width)
    node_table = jnp.concatenate([by_part, halo_table(by_part, halo_rows)], axis=1)

    def forward_part(operands):
        table_rows, own_rows, senders, receivers = operands
        send_proj = jnp.dot(table_rows, send_weight, preferred_element_type=jnp.float32)
        recv_proj = jnp.dot(own_rows, recv_weight, preferred_element_type=jnp.float32)
        pre_act = send_proj[senders] + recv_proj[receivers] + edge_bias
        return jax.ops.segment_sum(jax.nn.silu(pre_act), receivers, num_segments=NF_DEV)
    aggregate = lax.map(forward_part, (node_table, by_part, edge_sender, edge_receiver))
    hidden = (by_part.astype(jnp.float32) + aggregate / DEG).astype(jnp.bfloat16)
    coarse = restrict(hidden, owner_slot, slot_coarse) * 0.25
    coarse_low = coarse.astype(jnp.bfloat16)
    coarse_act = jnp.dot(coarse_low, coarse_weight, preferred_element_type=jnp.float32)
    coarse_mid = coarse + jax.nn.silu(coarse_act)
    top_scale = (NCC / (NC_DEV * DOMAINS)) ** 0.5
    top_level = jax.ops.segment_sum(coarse_mid, coarse_parent, num_segments=NCC) * top_scale
    top_act = jnp.dot(top_level, top_weight, precision=highest)
    coarse_out = (coarse_mid + jax.nn.silu(top_act)[coarse_parent]).astype(jnp.bfloat16)
    global_ids = (owner_slot // CAP * NC_DEV + cluster_index).reshape(-1)
    flat_hidden = hidden.reshape(-1, feature_width)
    joined = (flat_hidden.astype(jnp.float32) + coarse_out[global_ids].astype(jnp.float32)).astype(jnp.bfloat16)
    updated = jnp.dot(joined, out_weight, preferred_element_type=jnp.float32).astype(jnp.bfloat16)
    gscale = float(NF_DEV * DOMAINS) ** (-0.5)
    out_weight_grad = gscale * jnp.dot(joined.T, out_grad, preferred_element_type=jnp.float32)
    d_joined = jnp.dot(out_grad, out_weight.T, preferred_element_type=jnp.float32).astype(jnp.bfloat16)
    d_coarse_out = restrict(d_joined.reshape(DOMAINS, NF_DEV, feature_width), owner_slot, slot_coarse)
    d_top_act = jax.ops.segment_sum(d_coarse_out, coarse_parent, num_segments=NCC) * silu_grad(top_act)
    top_weight_grad = gscale * jnp.dot(top_level.T, d_top_act, precision=highest)
    d_top = jnp.dot(d_top_act, top_weight.T, precision=highest)
    d_coarse_mid = d_coarse_out + top_scale * d_top[coarse_parent]
    d_act = (d_coarse_mid * silu_grad(coarse_act)).astype(jnp.bfloat16)
    coarse_weight_grad = gscale * jnp.dot(coarse_low.T, d_act, preferred_element_type=jnp.float32)
    d_coarse = (d_coarse_mid + jnp.dot(d_act, coarse_weight.T, preferred_element_type=jnp.float32)).astype(jnp.bfloat16)
    d_hidden = d_joined.astype(jnp.float32) + 0.25 * d_coarse[global_ids].astype(jnp.float32)
    d_hidden = d_hidden.reshape(DOMAINS, NF_DEV, feature_width)

    def backward_part(operands):
        table_rows, own_rows, senders, receivers, d_rows = operands
        send_proj = jnp.dot(table_rows, send_weight, preferred_element_type=jnp.float32)
        recv_proj = jnp.dot(own_rows, recv_weight, preferred_element_type=jnp.float32)
        pre_act = send_proj[senders] + recv_proj[receivers] + edge_bias
        d_pre = (d_rows / DEG)[receivers] * silu_grad(pre_act)
        bias_term = lax.optimization_barrier(jnp.sum(d_pre, axis=0))
        d_send_proj = jax.ops.segment_sum(d_pre, senders, num_segments=table_rows.shape[0]).astype(jnp.bfloat16)
        d_recv_proj = jax.ops.segment_sum(d_pre, receivers, num_segments=NF_DEV).astype(jnp.bfloat16)
        send_term = jnp.dot(table_rows.T, d_send_proj, preferred_element_type=jnp.float32)
        recv_term = jnp.dot(own_rows.T, d_recv_proj, preferred_element_type=jnp.float32)
        d_table = jnp.dot(d_send_proj, send_weight.T, preferred_element_type=jnp.float32)
        d_local = jnp.dot(d_recv_proj, recv_weight.T, preferred_element_type=jnp.float32)
        local_grad = d_rows + d_table[:NF_DEV] + d_local
        return (bias_term, send_term, recv_term, local_grad, d_table[NF_DEV:].astype(jnp.bfloat16))
    bias_terms, send_terms, recv_terms, feature_grad, d_halo = lax.map(backward_part, (node_table, by_part, edge_sender, edge_receiver, d_hidden))
    d_halo = d_halo.reshape(DOMAINS, 4, SLOTS, feature_width)
    part_ids = jnp.arange(DOMAINS, dtype=jnp.int32)
    for direction, offset in enumerate(offset_list()):
        source = part_ids - offset
        present = (source >= 0) & (source < DOMAINS)
        clipped = jnp.clip(source, 0, DOMAINS - 1)
        block_values = jnp.where(present[:, None, None], d_halo[:, direction].astype(jnp.float32), jnp.zeros((), jnp.float32))
        feature_grad = feature_grad.at[clipped[:, None], halo_rows[clipped, direction]].add(block_values)
    send_weight_grad = gscale * lax.optimization_barrier(jnp.sum(send_terms, axis=0))
    recv_weight_grad = gscale * lax.optimization_barrier(jnp.sum(recv_terms, axis=0))
    edge_bias_grad = gscale * lax.optimization_barrier(jnp.sum(bias_terms, axis=0))
    return (updated, feature_grad.reshape(-1, feature_width), send_weight_grad, recv_weight_grad, edge_bias_grad, coarse_weight_grad, top_weight_grad, out_weight_grad)
```

```python
import functools

import jax
import jax.numpy as jnp
from jax import lax
from jax.experimental import pallas as pl
from jax.experimental.pallas import tpu as pltpu
from jax.sharding import PartitionSpec as P

DEG = 8
PW = 8
NCC = 256
OFFSETS = (1, -1, PW, -PW)
F32 = jnp.float32
BF16 = jnp.bfloat16


def mm(left, right):
    return lax.dot_general(left, right, (((1,), (0,)), ((), ())), preferred_element_type=F32)


def tn(left, right):
    return lax.dot_general(left, right, (((0,), (0,)), ((), ())), preferred_element_type=F32)


def nt(left, right):
    return lax.dot_general(left, right, (((1,), (1,)), ((), ())), preferred_element_type=F32)


def gate_of(values):
    return 0.5 * jnp.tanh(0.5 * values) + 0.5


def one_hot(ids, count):
    rows = lax.broadcasted_iota(jnp.int32, (count, ids.shape[1]), 0)
    return jnp.where(rows == ids, 1.0, 0.0).astype(BF16)


def kernel(
    domains, cap, block,
    feat, og, sw, rw, bias, cw, tw, ow, es, er, hr, osl, ci, cp,
    updated, fgrad, swg, rwg, bg, cwg, twg, owg,
    hsend, table, hots, sgrad, mt, dj, dpart, dland, dfull, ph, hid, cpart, cland, cfull,
    dhal, hret, wpart, wland, wfull, bmine, bland,
    halo_s, halo_r, ret_s, ret_r, stage_s, stage_r,
):
    me = lax.axis_index("dom")
    n = feat.shape[0]
    slots = hr.shape[2]
    ncd = cp.shape[0]
    nc = ncd * domains
    edges = es.shape[1]
    blocks = edges // block
    wrows = wland.shape[2]
    owners = n // wrows
    gscale = float(n * domains) ** (-0.5)
    top_scale = (NCC / nc) ** 0.5

    def to_peers(action):
        def body(i, carry):
            action(lax.rem(me + i, domains))
            return carry
        lax.fori_loop(1, domains, body, 0)

    def rdma(src, dst, s, r, peer):
        return pltpu.make_async_remote_copy(
            src_ref=src, dst_ref=dst, send_sem=s, recv_sem=r,
            device_id={"dom": peer}, device_id_type=pl.DeviceIdType.MESH,
        )

    def drain(ref, sem):
        pltpu.make_async_copy(ref, ref, sem).wait()

    def rows_of(ref, index, count):
        return ref.at[pl.ds(pl.multiple_of(index * count, count), count)]

    def scatter_start(part, land, k):
        def act(peer):
            rdma(rows_of(part, peer, ncd), land.at[me], stage_s.at[k], stage_r.at[k], peer).start()
        to_peers(act)
        land[me] = part[pl.ds(pl.multiple_of(me * ncd, ncd), ncd), :]

    def gather_start(full, k):
        mine = rows_of(full, me, ncd)

        def act(peer):
            rdma(mine, mine, stage_s.at[k], stage_r.at[k], peer).start()
        to_peers(act)

    def land_wait(land, k):
        drain(land.at[pl.ds(0, domains - 1)], stage_r.at[k])

    def full_wait(full, k):
        drain(full.at[pl.ds(0, (domains - 1) * ncd)], stage_r.at[k])

    def own_rows(full, values):
        full[pl.ds(pl.multiple_of(me * ncd, ncd), ncd), :] = values

    def w_scatter(m, k):
        def body(i, carry):
            peer = lax.rem(me + i, domains)

            @pl.when(peer < owners)
            def _():
                rdma(rows_of(wpart.at[m], peer, wrows), wland.at[m, me],
                     stage_s.at[k], stage_r.at[k], peer).start()
            return carry
        lax.fori_loop(1, domains, body, 0)

        @pl.when(me < owners)
        def _():
            wland[m, me] = wpart[m, pl.ds(pl.multiple_of(me * wrows, wrows), wrows), :]

    def w_gather(m, k, k2):
        @pl.when(me < owners)
        def _():
            drain(wland.at[m, pl.ds(0, domains - 1)], stage_r.at[k])
            total = jnp.sum(wland[m].astype(F32), axis=0)
            wfull[m, pl.ds(pl.multiple_of(me * wrows, wrows), wrows), :] = total.astype(BF16)
            mine = rows_of(wfull.at[m], me, wrows)

            def act(peer):
                rdma(mine, mine, stage_s.at[k2], stage_r.at[k2], peer).start()
            to_peers(act)

    def w_count(m, sem, few):
        if owners == domains:
            drain(wpart.at[m, pl.ds(0, few * wrows)], sem)
        else:
            @pl.when(me < owners)
            def _():
                drain(wpart.at[m, pl.ds(0, (owners - 1) * wrows)], sem)

            @pl.when(me >= owners)
            def _():
                drain(wpart.at[m], sem)

    def w_finish(m, k2, out):
        w_count(m, stage_r.at[k2], owners - 1)
        out[...] = gscale * wfull[m].astype(F32)

    barrier = pltpu.get_barrier_semaphore()
    to_peers(lambda peer: pl.semaphore_signal(
        barrier, inc=1, device_id={"dom": peer}, device_id_type=pl.DeviceIdType.MESH))

    features = feat[...]
    for k in range(4):
        hsend[k] = tn(one_hot(hr[0, k:k + 1, :], n), features).astype(BF16)
    owner = jnp.floor((osl[...].astype(F32) + 0.5) * (1.0 / cap)).astype(jnp.int32)
    mt[...] = one_hot(owner * ncd + ci[...], nc)
    d_joined = nt(og[...], ow[...]).astype(BF16)
    dj[...] = d_joined
    dpart[...] = mm(mt[...], d_joined).astype(BF16)
    tops = lax.broadcasted_iota(jnp.int32, (ncd, NCC), 1)
    own_rows(ph, jnp.where(tops == cp[...], 1.0, 0.0).astype(BF16))
    table[0:n, :] = features

    pl.semaphore_wait(barrier, domains - 1)

    def present(offset):
        other = me + offset
        return jnp.logical_and(other >= 0, other < domains)

    def halo_rows_at(ref, k):
        return ref.at[pl.ds(n + k * slots, slots)]

    for k, offset in enumerate(OFFSETS):
        @pl.when(present(offset))
        def _(k=k, offset=offset):
            rdma(hsend.at[k], halo_rows_at(table, k), halo_s.at[k], halo_r.at[k], me + offset).start()

        @pl.when(jnp.logical_not(present(-offset)))
        def _(k=k):
            table[n + k * slots:n + (k + 1) * slots, :] = jnp.zeros((slots, feat.shape[1]), BF16)
    scatter_start(dpart, dland, 0)
    gather_start(ph, 1)

    own_send = mm(features, sw[...])
    own_recv = mm(features, rw[...]) + bias[...]
    tr = n + 4 * slots
    for b in range(blocks):
        cols = slice(b * block, (b + 1) * block)
        hots[b, 0:tr, :] = one_hot(es[0:1, cols], tr)
        hots[b, tr:tr + n, :] = one_hot(er[0:1, cols], n)

    for k, offset in enumerate(OFFSETS):
        @pl.when(present(-offset))
        def _(k=k):
            drain(halo_rows_at(table, k), halo_r.at[k])
    halo_proj = mm(table[n:tr, :], sw[...])
    proj = jnp.concatenate([own_send, halo_proj, own_recv], axis=0).T.astype(BF16)

    aggregate = jnp.zeros((n, feat.shape[1]), F32)
    for b in range(blocks):
        pre = mm(proj, hots[b])
        gate = gate_of(pre)
        act = pre * gate
        sgrad[b] = (gate + act * (1.0 - gate)).astype(BF16)
        aggregate = aggregate + nt(hots[b, tr:tr + n, :], act.astype(BF16))
    hidden = (features.astype(F32) + aggregate * (1.0 / DEG)).astype(BF16)
    hid[...] = hidden
    cpart[...] = mm(mt[...], hidden).astype(BF16)
    scatter_start(cpart, cland, 2)

    land_wait(dland, 0)
    own_rows(dfull, jnp.sum(dland[...].astype(F32), axis=0).astype(BF16))
    gather_start(dfull, 3)

    land_wait(cland, 2)
    own_rows(cfull, (0.25 * jnp.sum(cland[...].astype(F32), axis=0)).astype(BF16))
    gather_start(cfull, 4)

    full_wait(ph, 1)
    full_wait(dfull, 3)
    parents = ph[...]
    d_out_low = dfull[...]
    d_top_sum = tn(parents, d_out_low)
    full_wait(cfull, 4)

    coarse_low = cfull[...]
    coarse_act = mm(coarse_low, cw[...])
    cgate = gate_of(coarse_act)
    csilu = coarse_act * cgate
    coarse_mid = coarse_low.astype(F32) + csilu
    top_low = (tn(parents, coarse_mid.astype(BF16)) * top_scale).astype(BF16)
    top_w = tw[...].astype(BF16)
    top_act = mm(top_low, top_w)
    tgate = gate_of(top_act)
    tsilu = top_act * tgate
    coarse_out = (coarse_mid + mm(parents, tsilu.astype(BF16))).astype(BF16)
    joined = (hid[...].astype(F32) + tn(mt[...], coarse_out)).astype(BF16)
    wpart[0] = tn(joined, og[...]).astype(BF16)
    w_scatter(0, 5)
    d_top_act = (d_top_sum * (tgate + tsilu * (1.0 - tgate))).astype(BF16)
    d_top = nt(d_top_act, top_w)
    d_mid = d_out_low.astype(F32) + top_scale * mm(parents, d_top.astype(BF16))
    d_act = (d_mid * (cgate + csilu * (1.0 - cgate))).astype(BF16)
    d_coarse = (d_mid + nt(d_act, cw[...])).astype(BF16)
    d_hidden = dj[...].astype(F32) + 0.25 * tn(mt[...], d_coarse)
    fgrad[...] = d_hidden
    d_agg = (d_hidden * (1.0 / DEG)).T.astype(BF16)

    d_proj = jnp.zeros((tr + n, feat.shape[1]), F32)
    for b in range(blocks):
        d_pre = mm(d_agg, hots[b, tr:tr + n, :]) * sgrad[b].astype(F32)
        d_proj = d_proj + nt(hots[b], d_pre.astype(BF16))
    d_send = d_proj[0:tr].astype(BF16)
    d_recv_full = d_proj[tr:tr + n]
    d_recv = d_recv_full.astype(BF16)
    bsum = jnp.sum(d_recv_full, axis=0, keepdims=True)
    bmine[...] = jnp.broadcast_to(bsum, bmine.shape)
    bland[me] = bmine[...]
    to_peers(lambda peer: rdma(bmine, bland.at[me], stage_s.at[7], stage_r.at[7], peer).start())
    wpart[1] = tn(table[...], d_send).astype(BF16)
    w_scatter(1, 8)
    wpart[2] = tn(features, d_recv).astype(BF16)
    w_scatter(2, 10)
    d_table = nt(d_send, sw[...])
    dhal[...] = d_table[n:tr].astype(BF16)
    for k, offset in enumerate(OFFSETS):
        rows = pl.ds(k * slots, slots)

        @pl.when(present(-offset))
        def _(k=k, offset=offset, rows=rows):
            rdma(dhal.at[rows], hret.at[rows], ret_s.at[k], ret_r.at[k], me - offset).start()

        @pl.when(jnp.logical_not(present(offset)))
        def _(k=k):
            hret[k * slots:(k + 1) * slots, :] = jnp.zeros((slots, feat.shape[1]), BF16)

    w_gather(0, 5, 6)
    fgrad[...] += d_table[0:n] + nt(d_recv, rw[...])
    updated[...] = mm(joined, ow[...]).astype(BF16)
    twg[...] = gscale * tn(top_low, d_top_act)
    cwg[...] = gscale * tn(coarse_low, d_act)
    w_gather(1, 8, 9)
    w_gather(2, 10, 11)
    for k, offset in enumerate(OFFSETS):
        @pl.when(present(offset))
        def _(k=k):
            drain(hret.at[pl.ds(k * slots, slots)], ret_r.at[k])
    back = jnp.zeros((n, feat.shape[1]), F32)
    for k in range(4):
        back = back + mm(one_hot(hr[0, k:k + 1, :], n), hret[k * slots:(k + 1) * slots, :])
    fgrad[...] += back
    drain(bland.at[pl.ds(0, domains - 1)], stage_r.at[7])
    bg[...] = gscale * jnp.sum(bland[...], axis=0)[0:1]
    w_finish(0, 6, owg)
    w_finish(1, 9, swg)
    w_finish(2, 11, rwg)

    for k, offset in enumerate(OFFSETS):
        @pl.when(present(offset))
        def _(k=k):
            drain(hsend.at[k], halo_s.at[k])

        @pl.when(present(-offset))
        def _(k=k):
            drain(dhal.at[pl.ds(k * slots, slots)], ret_s.at[k])
    for k in (0, 1, 2, 3, 4):
        full_like = dpart.at[pl.ds(0, (domains - 1) * ncd)]
        drain(full_like, stage_s.at[k])
    drain(bland.at[pl.ds(0, domains - 1)], stage_s.at[7])
    for m, k, k2 in ((0, 5, 6), (1, 8, 9), (2, 10, 11)):
        w_count(m, stage_s.at[k], owners - 1)

        @pl.when(me < owners)
        def _(m=m, k2=k2):
            drain(wland.at[m, pl.ds(0, domains - 1)], stage_s.at[k2])


def shards(
    features, out_grad, send_weight, recv_weight, edge_bias, coarse_weight, top_weight, out_weight,
    edge_sender, edge_receiver, halo_rows, owner_slot, cluster_index, slot_coarse, coarse_parent,
):
    domains = lax.axis_size("dom")
    n, h = features.shape
    ncd = coarse_parent.shape[0]
    nc = ncd * domains
    slots = halo_rows.shape[2]
    tr = n + 4 * slots
    edges = edge_sender.shape[1]
    block = min(edges, 512)
    blocks = edges // block
    cap = slot_coarse.shape[1] // domains
    wrows = max(16, n // domains)
    vmem = pl.BlockSpec(memory_space=pltpu.VMEM)
    dma = pltpu.SemaphoreType.DMA
    scratch = [
        pltpu.VMEM((4, slots, h), BF16),
        pltpu.VMEM((tr, h), BF16),
        pltpu.VMEM((blocks, tr + n, block), BF16),
        pltpu.VMEM((blocks, h, block), BF16),
        pltpu.VMEM((nc, n), BF16),
        pltpu.VMEM((n, h), BF16),
        pltpu.VMEM((nc, h), BF16),
        pltpu.VMEM((domains, ncd, h), BF16),
        pltpu.VMEM((nc, h), BF16),
        pltpu.VMEM((nc, NCC), BF16),
        pltpu.VMEM((n, h), BF16),
        pltpu.VMEM((nc, h), BF16),
        pltpu.VMEM((domains, ncd, h), BF16),
        pltpu.VMEM((nc, h), BF16),
        pltpu.VMEM((4 * slots, h), BF16),
        pltpu.VMEM((4 * slots, h), BF16),
        pltpu.VMEM((3, h, h), BF16),
        pltpu.VMEM((3, domains, wrows, h), BF16),
        pltpu.VMEM((3, h, h), BF16),
        pltpu.VMEM((8, h), F32),
        pltpu.VMEM((domains, 8, h), F32),
        dma((4,)), dma((4,)), dma((4,)), dma((4,)), dma((12,)), dma((12,)),
    ]
    big = jax.ShapeDtypeStruct((h, h), F32)
    outs = pl.pallas_call(
        functools.partial(kernel, domains, cap, block),
        out_shape=(
            jax.ShapeDtypeStruct((n, h), BF16),
            jax.ShapeDtypeStruct((n, h), F32),
            big, big, jax.ShapeDtypeStruct((1, h), F32), big, big, big,
        ),
        in_specs=[vmem] * 14,
        out_specs=[vmem] * 8,
        scratch_shapes=scratch,
        compiler_params=pltpu.CompilerParams(
            collective_id=0, has_side_effects=True, vmem_limit_bytes=56 * 1024 * 1024
        ),
    )(
        features, out_grad, send_weight, recv_weight, edge_bias.reshape(1, h), coarse_weight,
        top_weight, out_weight, edge_sender, edge_receiver, halo_rows, owner_slot, cluster_index,
        coarse_parent.reshape(ncd, 1),
    )
    return outs[:4] + (outs[4].reshape(h),) + outs[5:]


def solution(mesh):
    rows = P(("groups", "dom"), None)
    in_specs = (
        rows, rows, P(), P(), P(), P(), P(), P(), rows, rows,
        P(("groups", "dom"), None, None), rows, rows, rows, P(("groups", "dom")),
    )
    mat = P("groups", None)
    out_specs = (rows, rows, mat, mat, P("groups"), mat, mat, mat)
    return jax.shard_map(shards, mesh=mesh, in_specs=in_specs, out_specs=out_specs, check_vma=False)
```

```python
import functools

import jax
import jax.numpy as jnp
from jax import lax
from jax.experimental import pallas as pl
from jax.experimental.pallas import tpu as pltpu
from jax.sharding import PartitionSpec as P

DEG = 8
PW = 8
NCC = 256
OFFSETS = (1, -1, PW, -PW)
F32 = jnp.float32
BF16 = jnp.bfloat16


def mm(left, right):
    return lax.dot_general(left, right, (((1,), (0,)), ((), ())), preferred_element_type=F32)


def tn(left, right):
    return lax.dot_general(left, right, (((0,), (0,)), ((), ())), preferred_element_type=F32)


def nt(left, right):
    return lax.dot_general(left, right, (((1,), (1,)), ((), ())), preferred_element_type=F32)


def halves(values):
    high = values.astype(BF16)
    return high, (values - high.astype(F32)).astype(BF16)


def mm_exact(hot, values):
    high, low = halves(values)
    return mm(hot, high) + mm(hot, low)


def tn_exact(hot, values):
    high, low = halves(values)
    return tn(hot, high) + tn(hot, low)


def gate_of(values):
    return 0.5 * jnp.tanh(0.5 * values) + 0.5


def one_hot(ids, count):
    rows = lax.broadcasted_iota(jnp.int32, (count, ids.shape[1]), 0)
    return jnp.where(rows == ids, 1.0, 0.0).astype(BF16)


def kernel(
    domains, cap, block,
    feat, og, sw, rw, bias, cw, tw, ow, es, er, hr, osl, ci, cp,
    updated, fgrad, wfull, bg, cwg, twg,
    hsend, table, hots, sgrad, mt, dj, dpart, dland, dfull, ph, hid, cpart, cland, cfull,
    dhal, hret, wpart, wland, bmine, bland,
    halo_s, halo_r, ret_s, ret_r, stage_s, stage_r,
):
    me = lax.axis_index("dom")
    n = feat.shape[0]
    slots = hr.shape[2]
    ncd = cp.shape[1]
    nc = ncd * domains
    edges = es.shape[1]
    blocks = edges // block
    wrows = wland.shape[2]
    owners = n // wrows
    gscale = float(n * domains) ** (-0.5)
    top_scale = (NCC / nc) ** 0.5

    def to_peers(action):
        def body(i, carry):
            action(lax.rem(me + i, domains))
            return carry
        lax.fori_loop(1, domains, body, 0)

    def rdma(src, dst, s, r, peer):
        return pltpu.make_async_remote_copy(
            src_ref=src, dst_ref=dst, send_sem=s, recv_sem=r,
            device_id={"dom": peer}, device_id_type=pl.DeviceIdType.MESH,
        )

    def drain(ref, sem):
        pltpu.make_async_copy(ref, ref, sem).wait()

    def rows_of(ref, index, count):
        return ref.at[pl.ds(pl.multiple_of(index * count, count), count)]

    def scatter_start(part, land, k):
        def act(peer):
            rdma(rows_of(part, peer, ncd), land.at[me], stage_s.at[k], stage_r.at[k], peer).start()
        to_peers(act)
        land[me] = part[pl.ds(pl.multiple_of(me * ncd, ncd), ncd), :]

    def gather_start(full, k):
        mine = rows_of(full, me, ncd)

        def act(peer):
            rdma(mine, mine, stage_s.at[k], stage_r.at[k], peer).start()
        to_peers(act)

    def land_wait(land, k):
        drain(land.at[pl.ds(0, domains - 1)], stage_r.at[k])

    def full_wait(full, k):
        drain(full.at[pl.ds(0, (domains - 1) * ncd)], stage_r.at[k])

    def own_rows(full, values):
        full[pl.ds(pl.multiple_of(me * ncd, ncd), ncd), :] = values

    def w_scatter(m, k):
        def body(i, carry):
            peer = lax.rem(me + i, domains)

            @pl.when(peer < owners)
            def _():
                rdma(rows_of(wpart.at[m], peer, wrows), wland.at[m, me],
                     stage_s.at[k], stage_r.at[k], peer).start()
            return carry
        lax.fori_loop(1, domains, body, 0)

        @pl.when(me < owners)
        def _():
            wland[m, me] = wpart[m, pl.ds(pl.multiple_of(me * wrows, wrows), wrows), :]

    def w_gather(m, k, k2):
        @pl.when(me < owners)
        def _():
            drain(wland.at[m, pl.ds(0, domains - 1)], stage_r.at[k])
            total = jnp.sum(wland[m].astype(F32), axis=0)
            wfull[m, pl.ds(pl.multiple_of(me * wrows, wrows), wrows), :] = total.astype(BF16)
            mine = rows_of(wfull.at[m], me, wrows)

            def act(peer):
                rdma(mine, mine, stage_s.at[k2], stage_r.at[k2], peer).start()
            to_peers(act)

    def w_count(m, sem, few):
        if owners == domains:
            drain(wpart.at[m, pl.ds(0, few * wrows)], sem)
        else:
            @pl.when(me < owners)
            def _():
                drain(wpart.at[m, pl.ds(0, (owners - 1) * wrows)], sem)

            @pl.when(me >= owners)
            def _():
                drain(wpart.at[m], sem)

    def w_finish(m, k2):
        w_count(m, stage_r.at[k2], owners - 1)

    barrier = pltpu.get_barrier_semaphore()
    to_peers(lambda peer: pl.semaphore_signal(
        barrier, inc=1, device_id={"dom": peer}, device_id_type=pl.DeviceIdType.MESH))

    features = feat[...]
    for k in range(4):
        hsend[k] = tn(one_hot(hr[0, k:k + 1, :], n), features).astype(BF16)
    owner = jnp.floor((osl[...].astype(F32) + 0.5) * (1.0 / cap)).astype(jnp.int32)
    mt[...] = one_hot(owner * ncd + ci[...], nc)
    d_joined = nt(og[...], ow[...]).astype(BF16)
    dj[...] = d_joined
    dpart[...] = mm(mt[...], d_joined).astype(BF16)
    values = lax.broadcasted_iota(jnp.int32, (NCC, 128), 0).astype(F32).astype(BF16)
    own_rows(ph, tn(one_hot(cp[...], NCC), values).astype(BF16))
    table[0:n, :] = features

    pl.semaphore_wait(barrier, domains - 1)

    def present(offset):
        other = me + offset
        return jnp.logical_and(other >= 0, other < domains)

    def halo_rows_at(ref, k):
        return ref.at[pl.ds(n + k * slots, slots)]

    for k, offset in enumerate(OFFSETS):
        @pl.when(present(offset))
        def _(k=k, offset=offset):
            rdma(hsend.at[k], halo_rows_at(table, k), halo_s.at[k], halo_r.at[k], me + offset).start()

        @pl.when(jnp.logical_not(present(-offset)))
        def _(k=k):
            table[n + k * slots:n + (k + 1) * slots, :] = jnp.zeros((slots, feat.shape[1]), BF16)
    scatter_start(dpart, dland, 0)
    gather_start(ph, 1)

    own_send = mm(features, sw[...])
    own_recv = mm(features, rw[...]) + bias[...]
    tr = n + 4 * slots
    for b in range(blocks):
        cols = slice(b * block, (b + 1) * block)
        hots[b, 0:tr, :] = one_hot(es[0:1, cols], tr)
        hots[b, tr:tr + n, :] = one_hot(er[0:1, cols], n)

    for k, offset in enumerate(OFFSETS):
        @pl.when(present(-offset))
        def _(k=k):
            drain(halo_rows_at(table, k), halo_r.at[k])
    halo_proj = mm(table[n:tr, :], sw[...])
    proj = jnp.concatenate([own_send, halo_proj, own_recv], axis=0).T.astype(BF16)

    aggregate = jnp.zeros((n, feat.shape[1]), F32)
    for b in range(blocks):
        pre = mm(proj, hots[b])
        gate = gate_of(pre)
        act = pre * gate
        sgrad[b] = (gate + act * (1.0 - gate)).astype(BF16)
        aggregate = aggregate + nt(hots[b, tr:tr + n, :], act.astype(BF16))
    hidden = (features.astype(F32) + aggregate * (1.0 / DEG)).astype(BF16)
    hid[...] = hidden
    cpart[...] = mm(mt[...], hidden).astype(BF16)
    scatter_start(cpart, cland, 2)

    land_wait(dland, 0)
    own_rows(dfull, jnp.sum(dland[...].astype(F32), axis=0).astype(BF16))
    gather_start(dfull, 3)

    land_wait(cland, 2)
    own_rows(cfull, 0.25 * jnp.sum(cland[...].astype(F32), axis=0))
    gather_start(cfull, 4)

    full_wait(ph, 1)
    full_wait(dfull, 3)
    lanes = lax.broadcasted_iota(jnp.int32, (nc, NCC), 1).astype(F32)
    ids = ph[...].astype(F32)
    ids = jnp.concatenate([ids] * (NCC // 128), axis=1)
    parents = jnp.where(lanes == ids, 1.0, 0.0).astype(BF16)
    d_out = dfull[...].astype(F32)
    d_top_sum = tn(parents, dfull[...])
    full_wait(cfull, 4)

    coarse = cfull[...]
    coarse_low = coarse.astype(BF16)
    coarse_act = mm(coarse_low, cw[...])
    cgate = gate_of(coarse_act)
    csilu = coarse_act * cgate
    coarse_mid = coarse + csilu
    top_level = tn_exact(parents, coarse_mid) * top_scale
    top_hi, top_lo = halves(top_level)
    w_hi, w_lo = halves(tw[...])
    top_act = mm(top_hi, w_hi) + (mm(top_hi, w_lo) + mm(top_lo, w_hi))
    tgate = gate_of(top_act)
    tsilu = top_act * tgate
    coarse_out = (coarse_mid + mm_exact(parents, tsilu)).astype(BF16)
    joined = (hid[...].astype(F32) + tn(mt[...], coarse_out)).astype(BF16)
    wpart[0] = tn(joined, og[...]).astype(BF16)
    w_scatter(0, 5)
    d_top_act = d_top_sum * (tgate + tsilu * (1.0 - tgate))
    dt_hi, dt_lo = halves(d_top_act)
    d_top = nt(dt_hi, w_hi) + (nt(dt_hi, w_lo) + nt(dt_lo, w_hi))
    d_mid = d_out + top_scale * mm_exact(parents, d_top)
    d_act = (d_mid * (cgate + csilu * (1.0 - cgate))).astype(BF16)
    d_coarse = (d_mid + nt(d_act, cw[...])).astype(BF16)
    d_hidden = dj[...].astype(F32) + 0.25 * tn(mt[...], d_coarse)
    fgrad[...] = d_hidden
    d_agg = (d_hidden * (1.0 / DEG)).T.astype(BF16)

    d_proj = jnp.zeros((tr + n, feat.shape[1]), F32)
    for b in range(blocks):
        d_pre = mm(d_agg, hots[b, tr:tr + n, :]) * sgrad[b].astype(F32)
        d_proj = d_proj + nt(hots[b], d_pre.astype(BF16))
    d_send = d_proj[0:tr].astype(BF16)
    d_recv_full = d_proj[tr:tr + n]
    d_recv = d_recv_full.astype(BF16)
    bsum = jnp.sum(d_recv_full, axis=0, keepdims=True)
    bmine[...] = bsum
    bland[me] = bmine[...]
    to_peers(lambda peer: rdma(bmine, bland.at[me], stage_s.at[7], stage_r.at[7], peer).start())
    wpart[1] = tn(table[...], d_send).astype(BF16)
    w_scatter(1, 8)
    wpart[2] = tn(features, d_recv).astype(BF16)
    w_scatter(2, 10)
    d_table = nt(d_send, sw[...])
    dhal[...] = d_table[n:tr].astype(BF16)
    for k, offset in enumerate(OFFSETS):
        rows = pl.ds(k * slots, slots)

        @pl.when(present(-offset))
        def _(k=k, offset=offset, rows=rows):
            rdma(dhal.at[rows], hret.at[rows], ret_s.at[k], ret_r.at[k], me - offset).start()

        @pl.when(jnp.logical_not(present(offset)))
        def _(k=k):
            hret[k * slots:(k + 1) * slots, :] = jnp.zeros((slots, feat.shape[1]), BF16)

    w_gather(0, 5, 6)
    fgrad[...] += d_table[0:n] + nt(d_recv, rw[...])
    updated[...] = mm(joined, ow[...]).astype(BF16)
    twg[...] = gscale * (tn(top_hi, dt_hi) + (tn(top_hi, dt_lo) + tn(top_lo, dt_hi)))
    cwg[...] = gscale * tn(coarse_low, d_act)
    w_gather(1, 8, 9)
    w_gather(2, 10, 11)
    for k, offset in enumerate(OFFSETS):
        @pl.when(present(offset))
        def _(k=k):
            drain(hret.at[pl.ds(k * slots, slots)], ret_r.at[k])
    back = jnp.zeros((n, feat.shape[1]), F32)
    for k in range(4):
        back = back + mm(one_hot(hr[0, k:k + 1, :], n), hret[k * slots:(k + 1) * slots, :])
    fgrad[...] += back
    drain(bland.at[pl.ds(0, domains - 1)], stage_r.at[7])
    bg[...] = gscale * jnp.sum(bland[...], axis=0)
    w_finish(0, 6)
    w_finish(1, 9)
    w_finish(2, 11)

    for k, offset in enumerate(OFFSETS):
        @pl.when(present(offset))
        def _(k=k):
            drain(hsend.at[k], halo_s.at[k])

        @pl.when(present(-offset))
        def _(k=k):
            drain(dhal.at[pl.ds(k * slots, slots)], ret_s.at[k])
    for ref, k in ((dpart, 0), (ph, 1), (cpart, 2), (dfull, 3), (cfull, 4)):
        drain(ref.at[pl.ds(0, (domains - 1) * ncd)], stage_s.at[k])
    drain(bland.at[pl.ds(0, domains - 1)], stage_s.at[7])
    for m, k, k2 in ((0, 5, 6), (1, 8, 9), (2, 10, 11)):
        w_count(m, stage_s.at[k], owners - 1)

        @pl.when(me < owners)
        def _(m=m, k2=k2):
            drain(wland.at[m, pl.ds(0, domains - 1)], stage_s.at[k2])


def finish(
    gscale, updated_in, fgrad_in, wfull, bias_in, coarse_in, top_in,
    updated, fgrad, swg, rwg, bg, cwg, twg, owg,
):
    updated[...] = updated_in[...]
    fgrad[...] = fgrad_in[...]
    owg[...] = gscale * wfull[0].astype(F32)
    swg[...] = gscale * wfull[1].astype(F32)
    rwg[...] = gscale * wfull[2].astype(F32)
    bg[...] = bias_in[...]
    cwg[...] = coarse_in[...]
    twg[...] = top_in[...]


def shards(
    features, out_grad, send_weight, recv_weight, edge_bias, coarse_weight, top_weight, out_weight,
    edge_sender, edge_receiver, halo_rows, owner_slot, cluster_index, slot_coarse, coarse_parent,
):
    domains = lax.axis_size("dom")
    n, h = features.shape
    ncd = coarse_parent.shape[0]
    nc = ncd * domains
    slots = halo_rows.shape[2]
    tr = n + 4 * slots
    edges = edge_sender.shape[1]
    block = min(edges, 512)
    blocks = edges // block
    cap = slot_coarse.shape[1] // domains
    wrows = max(16, n // domains)
    vmem = pl.BlockSpec(memory_space=pltpu.VMEM)
    dma = pltpu.SemaphoreType.DMA
    scratch = [
        pltpu.VMEM((4, slots, h), BF16),
        pltpu.VMEM((tr, h), BF16),
        pltpu.VMEM((blocks, tr + n, block), BF16),
        pltpu.VMEM((blocks, h, block), BF16),
        pltpu.VMEM((nc, n), BF16),
        pltpu.VMEM((n, h), BF16),
        pltpu.VMEM((nc, h), BF16),
        pltpu.VMEM((domains, ncd, h), BF16),
        pltpu.VMEM((nc, h), BF16),
        pltpu.VMEM((nc, 128), BF16),
        pltpu.VMEM((n, h), BF16),
        pltpu.VMEM((nc, h), BF16),
        pltpu.VMEM((domains, ncd, h), BF16),
        pltpu.VMEM((nc, h), F32),
        pltpu.VMEM((4 * slots, h), BF16),
        pltpu.VMEM((4 * slots, h), BF16),
        pltpu.VMEM((3, h, h), BF16),
        pltpu.VMEM((3, domains, wrows, h), BF16),
        pltpu.VMEM((1, h), F32),
        pltpu.VMEM((domains, 1, h), F32),
        dma((4,)), dma((4,)), dma((4,)), dma((4,)), dma((12,)), dma((12,)),
    ]
    big = jax.ShapeDtypeStruct((h, h), F32)
    outs = pl.pallas_call(
        functools.partial(kernel, domains, cap, block),
        out_shape=(
            jax.ShapeDtypeStruct((n, h), BF16),
            jax.ShapeDtypeStruct((n, h), F32),
            jax.ShapeDtypeStruct((3, h, h), BF16), jax.ShapeDtypeStruct((1, h), F32), big, big,
        ),
        in_specs=[vmem] * 14,
        out_specs=[vmem] * 6,
        scratch_shapes=scratch,
        compiler_params=pltpu.CompilerParams(
            collective_id=0, has_side_effects=True, vmem_limit_bytes=56 * 1024 * 1024
        ),
    )(
        features, out_grad, send_weight, recv_weight, edge_bias.reshape(1, h), coarse_weight,
        top_weight, out_weight, edge_sender, edge_receiver, halo_rows, owner_slot, cluster_index,
        coarse_parent.reshape(1, ncd),
    )
    outs = pl.pallas_call(
        functools.partial(finish, float(n * domains) ** (-0.5)),
        out_shape=(
            jax.ShapeDtypeStruct((n, h), BF16),
            jax.ShapeDtypeStruct((n, h), F32),
            big, big, jax.ShapeDtypeStruct((1, h), F32), big, big, big,
        ),
        in_specs=[vmem] * 6,
        out_specs=[vmem] * 8,
        compiler_params=pltpu.CompilerParams(vmem_limit_bytes=60 * 1024 * 1024),
    )(*outs)
    return outs[:4] + (outs[4].reshape(h),) + outs[5:]


def solution(mesh):
    rows = P(("groups", "dom"), None)
    in_specs = (
        rows, rows, P(), P(), P(), P(), P(), P(), rows, rows,
        P(("groups", "dom"), None, None), rows, rows, rows, P(("groups", "dom")),
    )
    mat = P("groups", None)
    out_specs = (rows, rows, mat, mat, P("groups"), mat, mat, mat)
    return jax.shard_map(shards, mesh=mesh, in_specs=in_specs, out_specs=out_specs, check_vma=False)
```

```python
import functools

import jax
import jax.numpy as jnp
from jax import lax
from jax.experimental import pallas as pl
from jax.experimental.pallas import tpu as pltpu
from jax.sharding import PartitionSpec as P

DEG = 8
PW = 8
NCC = 256
OFFSETS = (1, -1, PW, -PW)
F32 = jnp.float32
BF16 = jnp.bfloat16


def mm(left, right):
    return lax.dot_general(left, right, (((1,), (0,)), ((), ())), preferred_element_type=F32)


def tn(left, right):
    return lax.dot_general(left, right, (((0,), (0,)), ((), ())), preferred_element_type=F32)


def nt(left, right):
    return lax.dot_general(left, right, (((1,), (1,)), ((), ())), preferred_element_type=F32)


def halves(values):
    high = values.astype(BF16)
    return high, (values - high.astype(F32)).astype(BF16)


def mm_exact(hot, values):
    high, low = halves(values)
    return mm(hot, high) + mm(hot, low)


def tn_exact(hot, values):
    high, low = halves(values)
    return tn(hot, high) + tn(hot, low)


def gate_of(values):
    return 0.5 * jnp.tanh(0.5 * values) + 0.5


def one_hot(ids, count):
    rows = lax.broadcasted_iota(jnp.int32, (count, ids.shape[1]), 0)
    return jnp.where(rows == ids, 1.0, 0.0).astype(BF16)


def kernel(
    domains, cap, block,
    feat, og, sw, rw, bias, cw, tw, ow, es, er, hr, osl, ci, cp,
    updated, fgrad, wf0, wf1, wf2, bg, cwg, twg,
    hsend, table, hots, sgrad, mt, dj, dpart, dpl, dps, dland, dfull, ph, hid, cpart, cpl, cps, cland, cfull,
    dhal, hret, wp0, wp1, wp2, wq0, wq1, wq2, ws0, ws1, ws2, wl0, wl1, wl2, bmine, bland,
    halo_s, halo_r, ret_s, ret_r, stage_s, stage_r,
):
    me = lax.axis_index("dom")
    n = feat.shape[0]
    slots = hr.shape[2]
    ncd = cp.shape[1]
    h = feat.shape[1]
    wrows = wl0.shape[1]
    wparts, wplands, wpsums = (wp0, wp1, wp2), (wq0, wq1, wq2), (ws0, ws1, ws2)
    wlands, wfulls = (wl0, wl1, wl2), (wf0, wf1, wf2)
    nc = ncd * domains
    edges = es.shape[1]
    blocks = edges // block
    gscale = float(n * domains) ** (-0.5)
    top_scale = (NCC / nc) ** 0.5

    def to_peers(action):
        def body(i, carry):
            action(lax.rem(me + i, domains))
            return carry
        lax.fori_loop(1, domains, body, 0)

    def rdma(src, dst, s, r, peer):
        return pltpu.make_async_remote_copy(
            src_ref=src, dst_ref=dst, send_sem=s, recv_sem=r,
            device_id={"dom": peer}, device_id_type=pl.DeviceIdType.MESH,
        )

    def drain(ref, sem):
        pltpu.make_async_copy(ref, ref, sem).wait()

    half = domains // 2
    slot = lax.div(me, 2)
    par = lax.rem(me, 2)
    partner = me + 1 - 2 * par
    wown = h // wrows // 2

    def piece(start, count):
        return pl.ds(pl.multiple_of(start * count, count), count)

    def if_owner(oh, action):
        if oh == half:
            action()
        else:
            pl.when(slot < oh)(action)

    def same_parity(action):
        def body(i, carry):
            other = lax.rem(slot + i, half)
            action(other, 2 * other + par)
            return carry
        lax.fori_loop(1, half, body, 0)

    def pair_start(part, pland, k):
        rows = pland.shape[0]
        rdma(part.at[piece(1 - par, rows)], pland, stage_s.at[4 * k], stage_r.at[4 * k], partner).start()

    def scatter_start(part, pland, psum, land, k, oh):
        rows, count = pland.shape[0], land.shape[1]
        drain(pland, stage_r.at[4 * k])
        psum[...] = (part[piece(par, rows), :] + pland[...]).astype(BF16)

        def act(other, peer):
            def go():
                rdma(psum.at[piece(other, count)], land.at[slot],
                     stage_s.at[4 * k + 1], stage_r.at[4 * k + 1], peer).start()
            if oh == half:
                go()
            else:
                pl.when(other < oh)(go)
        same_parity(act)

        def own():
            land[slot] = psum[piece(slot, count), :]
        if_owner(oh, own)

    def land_sum(land, k):
        drain(land.at[pl.ds(0, half - 1)], stage_r.at[4 * k + 1])
        return jnp.sum(land[...].astype(F32), axis=0)

    def gather_start(full, values, k, oh):
        count = values.shape[0]
        index = par * oh + slot
        full[piece(index, count), :] = values
        mine = full.at[piece(index, count)]
        same_parity(lambda other, peer: rdma(
            mine, mine, stage_s.at[4 * k + 2], stage_r.at[4 * k + 2], peer).start())

    def block_drain(ref, sem, oh, count):
        if oh == half:
            drain(ref.at[pl.ds(0, (oh - 1) * count)], sem)
        else:
            @pl.when(slot < oh)
            def _():
                drain(ref.at[pl.ds(0, (oh - 1) * count)], sem)

            @pl.when(slot >= oh)
            def _():
                drain(ref.at[pl.ds(0, oh * count)], sem)

    def forward(full, k, oh, count):
        rows = oh * count
        block_drain(full, stage_r.at[4 * k + 2], oh, count)
        mine = full.at[piece(par, rows)]
        rdma(mine, mine, stage_s.at[4 * k + 3], stage_r.at[4 * k + 3], partner).start()

    def full_wait(full, k, oh, count):
        drain(full.at[pl.ds(0, oh * count)], stage_r.at[4 * k + 3])

    def w_gather(m):
        def act():
            gather_start(wfulls[m], land_sum(wlands[m], 2 + m).astype(BF16), 2 + m, wown)
        if_owner(wown, act)

    barrier = pltpu.get_barrier_semaphore()
    to_peers(lambda peer: pl.semaphore_signal(
        barrier, inc=1, device_id={"dom": peer}, device_id_type=pl.DeviceIdType.MESH))

    features = feat[...]
    for k in range(4):
        hsend[k] = tn(one_hot(hr[0, k:k + 1, :], n), features).astype(BF16)
    owner = jnp.floor((osl[...].astype(F32) + 0.5) * (1.0 / cap))
    chip = jnp.floor(owner * 0.5)
    place = (owner - 2.0 * chip) * half + chip
    mt[...] = one_hot(place.astype(jnp.int32) * ncd + ci[...], nc)
    d_joined = nt(og[...], ow[...]).astype(BF16)
    dj[...] = d_joined
    dpart[...] = mm(mt[...], d_joined)
    values = lax.broadcasted_iota(jnp.int32, (NCC, 128), 0).astype(F32).astype(BF16)
    my_parents = tn(one_hot(cp[...], NCC), values).astype(BF16)
    table[0:n, :] = features

    pl.semaphore_wait(barrier, domains - 1)

    def present(offset):
        other = me + offset
        return jnp.logical_and(other >= 0, other < domains)

    def halo_rows_at(ref, k):
        return ref.at[pl.ds(n + k * slots, slots)]

    for k, offset in enumerate(OFFSETS):
        @pl.when(present(offset))
        def _(k=k, offset=offset):
            rdma(hsend.at[k], halo_rows_at(table, k), halo_s.at[k], halo_r.at[k], me + offset).start()

        @pl.when(jnp.logical_not(present(-offset)))
        def _(k=k):
            table[n + k * slots:n + (k + 1) * slots, :] = jnp.zeros((slots, feat.shape[1]), BF16)
    pair_start(dpart, dpl, 0)
    gather_start(ph, my_parents, 5, half)

    own_send = mm(features, sw[...])
    own_recv = mm(features, rw[...]) + bias[...]
    tr = n + 4 * slots
    for b in range(blocks):
        cols = slice(b * block, (b + 1) * block)
        hots[b, 0:tr, :] = one_hot(es[0:1, cols], tr)
        hots[b, tr:tr + n, :] = one_hot(er[0:1, cols], n)

    scatter_start(dpart, dpl, dps, dland, 0, half)
    for k, offset in enumerate(OFFSETS):
        @pl.when(present(-offset))
        def _(k=k):
            drain(halo_rows_at(table, k), halo_r.at[k])
    halo_proj = mm(table[n:tr, :], sw[...])
    proj = jnp.concatenate([own_send, halo_proj, own_recv], axis=0).T.astype(BF16)

    aggregate = jnp.zeros((n, feat.shape[1]), F32)
    for b in range(blocks):
        pre = mm(proj, hots[b])
        gate = gate_of(pre)
        act = pre * gate
        sgrad[b] = (gate + act * (1.0 - gate)).astype(BF16)
        aggregate = aggregate + nt(hots[b, tr:tr + n, :], act.astype(BF16))
    hidden = (features.astype(F32) + aggregate * (1.0 / DEG)).astype(BF16)
    hid[...] = hidden
    cpart[...] = mm(mt[...], hidden)
    pair_start(cpart, cpl, 1)
    forward(ph, 5, half, ncd)
    d_own = land_sum(dland, 0).astype(BF16)
    scatter_start(cpart, cpl, cps, cland, 1, half)
    gather_start(dfull, d_own, 0, half)
    gather_start(cfull, 0.25 * land_sum(cland, 1), 1, half)
    forward(dfull, 0, half, ncd)
    full_wait(ph, 5, half, ncd)
    lanes = lax.broadcasted_iota(jnp.int32, (nc, NCC), 1).astype(F32)
    ids = ph[...].astype(F32)
    ids = jnp.concatenate([ids] * (NCC // 128), axis=1)
    parents = jnp.where(lanes == ids, 1.0, 0.0).astype(BF16)
    full_wait(dfull, 0, half, ncd)
    forward(cfull, 1, half, ncd)
    d_out = dfull[...].astype(F32)
    d_top_sum = tn(parents, dfull[...])
    full_wait(cfull, 1, half, ncd)

    coarse = cfull[...]
    coarse_low = coarse.astype(BF16)
    coarse_act = mm(coarse_low, cw[...])
    cgate = gate_of(coarse_act)
    csilu = coarse_act * cgate
    coarse_mid = coarse + csilu
    top_level = tn_exact(parents, coarse_mid) * top_scale
    top_hi, top_lo = halves(top_level)
    w_hi, w_lo = halves(tw[...])
    top_act = mm(top_hi, w_hi) + (mm(top_hi, w_lo) + mm(top_lo, w_hi))
    tgate = gate_of(top_act)
    tsilu = top_act * tgate
    coarse_out = (coarse_mid + mm_exact(parents, tsilu)).astype(BF16)
    joined = (hid[...].astype(F32) + tn(mt[...], coarse_out)).astype(BF16)
    wp0[...] = tn(joined, og[...])
    pair_start(wp0, wq0, 2)
    d_top_act = d_top_sum * (tgate + tsilu * (1.0 - tgate))
    dt_hi, dt_lo = halves(d_top_act)
    d_top = nt(dt_hi, w_hi) + (nt(dt_hi, w_lo) + nt(dt_lo, w_hi))
    d_mid = d_out + top_scale * mm_exact(parents, d_top)
    d_act = (d_mid * (cgate + csilu * (1.0 - cgate))).astype(BF16)
    d_coarse = (d_mid + nt(d_act, cw[...])).astype(BF16)
    scatter_start(wparts[0], wplands[0], wpsums[0], wlands[0], 2 + 0, wown)
    d_hidden = dj[...].astype(F32) + 0.25 * tn(mt[...], d_coarse)
    fgrad[...] = d_hidden
    d_agg = (d_hidden * (1.0 / DEG)).T.astype(BF16)

    d_proj = jnp.zeros((tr + n, feat.shape[1]), F32)
    for b in range(blocks):
        d_pre = mm(d_agg, hots[b, tr:tr + n, :]) * sgrad[b].astype(F32)
        d_proj = d_proj + nt(hots[b], d_pre.astype(BF16))
    d_send = d_proj[0:tr].astype(BF16)
    d_recv_full = d_proj[tr:tr + n]
    d_recv = d_recv_full.astype(BF16)
    bsum = jnp.sum(d_recv_full, axis=0, keepdims=True)
    bmine[...] = bsum
    bland[me] = bmine[...]
    to_peers(lambda peer: rdma(bmine, bland.at[me], stage_s.at[24], stage_r.at[24], peer).start())
    wp1[...] = tn(table[...], d_send)
    pair_start(wp1, wq1, 3)
    wp2[...] = tn(features, d_recv)
    pair_start(wp2, wq2, 4)
    d_table = nt(d_send, sw[...])
    dhal[...] = d_table[n:tr].astype(BF16)
    for k, offset in enumerate(OFFSETS):
        rows = pl.ds(k * slots, slots)

        @pl.when(present(-offset))
        def _(k=k, offset=offset, rows=rows):
            rdma(dhal.at[rows], hret.at[rows], ret_s.at[k], ret_r.at[k], me - offset).start()

        @pl.when(jnp.logical_not(present(offset)))
        def _(k=k):
            hret[k * slots:(k + 1) * slots, :] = jnp.zeros((slots, feat.shape[1]), BF16)

    scatter_start(wparts[1], wplands[1], wpsums[1], wlands[1], 2 + 1, wown)
    scatter_start(wparts[2], wplands[2], wpsums[2], wlands[2], 2 + 2, wown)
    w_gather(0)
    fgrad[...] += d_table[0:n] + nt(d_recv, rw[...])
    updated[...] = mm(joined, ow[...]).astype(BF16)
    twg[...] = gscale * (tn(top_hi, dt_hi) + (tn(top_hi, dt_lo) + tn(top_lo, dt_hi)))
    cwg[...] = gscale * tn(coarse_low, d_act)
    w_gather(1)
    w_gather(2)
    forward(wf0, 2, wown, wrows)
    for k, offset in enumerate(OFFSETS):
        @pl.when(present(offset))
        def _(k=k):
            drain(hret.at[pl.ds(k * slots, slots)], ret_r.at[k])
    back = jnp.zeros((n, feat.shape[1]), F32)
    for k in range(4):
        back = back + mm(one_hot(hr[0, k:k + 1, :], n), hret[k * slots:(k + 1) * slots, :])
    fgrad[...] += back
    drain(bland.at[pl.ds(0, domains - 1)], stage_r.at[24])
    bg[...] = gscale * jnp.sum(bland[...], axis=0)
    forward(wf1, 3, wown, wrows)
    forward(wf2, 4, wown, wrows)
    for m in range(3):
        full_wait(wfulls[m], 2 + m, wown, wrows)

    for k, offset in enumerate(OFFSETS):
        @pl.when(present(offset))
        def _(k=k):
            drain(hsend.at[k], halo_s.at[k])

        @pl.when(present(-offset))
        def _(k=k):
            drain(dhal.at[pl.ds(k * slots, slots)], ret_s.at[k])
    stages = [(dpl, dps, dland, dfull, half, ncd, 0), (cpl, cps, cland, cfull, half, ncd, 1)]
    for m in range(3):
        stages.append((wplands[m], wpsums[m], wlands[m], wfulls[m], wown, wrows, 2 + m))
    for pland, psum, land, full, oh, count, k in stages:
        drain(pland, stage_s.at[4 * k])
        block_drain(psum, stage_s.at[4 * k + 1], oh, count)
    stages.append((None, None, None, ph, half, ncd, 5))
    for pland, psum, land, full, oh, count, k in stages:
        def sent(full=full, land=land, oh=oh, count=count, k=k):
            if oh == half:
                drain(full.at[pl.ds(0, (half - 1) * count)], stage_s.at[4 * k + 2])
            else:
                drain(land.at[pl.ds(0, half - 1)], stage_s.at[4 * k + 2])
        if_owner(oh, sent)
        drain(full.at[pl.ds(0, oh * count)], stage_s.at[4 * k + 3])
    drain(bland.at[pl.ds(0, domains - 1)], stage_s.at[24])


def finish(
    gscale, updated_in, fgrad_in, w0, w1, w2, bias_in, coarse_in, top_in,
    updated, fgrad, swg, rwg, bg, cwg, twg, owg,
):
    updated[...] = updated_in[...]
    fgrad[...] = fgrad_in[...]
    owg[...] = gscale * w0[...].astype(F32)
    swg[...] = gscale * w1[...].astype(F32)
    rwg[...] = gscale * w2[...].astype(F32)
    bg[...] = bias_in[...]
    cwg[...] = coarse_in[...]
    twg[...] = top_in[...]


def shards(
    features, out_grad, send_weight, recv_weight, edge_bias, coarse_weight, top_weight, out_weight,
    edge_sender, edge_receiver, halo_rows, owner_slot, cluster_index, slot_coarse, coarse_parent,
):
    domains = lax.axis_size("dom")
    n, h = features.shape
    ncd = coarse_parent.shape[0]
    nc = ncd * domains
    slots = halo_rows.shape[2]
    tr = n + 4 * slots
    edges = edge_sender.shape[1]
    block = min(edges, 512)
    blocks = edges // block
    cap = slot_coarse.shape[1] // domains
    wrows = max(16, h // domains)
    vmem = pl.BlockSpec(memory_space=pltpu.VMEM)
    dma = pltpu.SemaphoreType.DMA
    scratch = [
        pltpu.VMEM((4, slots, h), BF16),
        pltpu.VMEM((tr, h), BF16),
        pltpu.VMEM((blocks, tr + n, block), BF16),
        pltpu.VMEM((blocks, h, block), BF16),
        pltpu.VMEM((nc, n), BF16),
        pltpu.VMEM((n, h), BF16),
        pltpu.VMEM((nc, h), F32),
        pltpu.VMEM((nc // 2, h), F32),
        pltpu.VMEM((nc // 2, h), BF16),
        pltpu.VMEM((domains // 2, ncd, h), BF16),
        pltpu.VMEM((nc, h), BF16),
        pltpu.VMEM((nc, 128), BF16),
        pltpu.VMEM((n, h), BF16),
        pltpu.VMEM((nc, h), F32),
        pltpu.VMEM((nc // 2, h), F32),
        pltpu.VMEM((nc // 2, h), BF16),
        pltpu.VMEM((domains // 2, ncd, h), BF16),
        pltpu.VMEM((nc, h), F32),
        pltpu.VMEM((4 * slots, h), BF16),
        pltpu.VMEM((4 * slots, h), BF16),
        *[pltpu.VMEM((h, h), F32)] * 3,
        *[pltpu.VMEM((h // 2, h), F32)] * 3,
        *[pltpu.VMEM((h // 2, h), BF16)] * 3,
        *[pltpu.VMEM((domains // 2, wrows, h), BF16)] * 3,
        pltpu.VMEM((1, h), F32),
        pltpu.VMEM((domains, 1, h), F32),
        dma((4,)), dma((4,)), dma((4,)), dma((4,)), dma((25,)), dma((25,)),
    ]
    big = jax.ShapeDtypeStruct((h, h), F32)
    outs = pl.pallas_call(
        functools.partial(kernel, domains, cap, block),
        out_shape=(
            jax.ShapeDtypeStruct((n, h), BF16),
            jax.ShapeDtypeStruct((n, h), F32),
            *[jax.ShapeDtypeStruct((h, h), BF16)] * 3, jax.ShapeDtypeStruct((1, h), F32), big, big,
        ),
        in_specs=[vmem] * 14,
        out_specs=[vmem] * 8,
        scratch_shapes=scratch,
        compiler_params=pltpu.CompilerParams(
            collective_id=0, has_side_effects=True, vmem_limit_bytes=56 * 1024 * 1024
        ),
    )(
        features, out_grad, send_weight, recv_weight, edge_bias.reshape(1, h), coarse_weight,
        top_weight, out_weight, edge_sender, edge_receiver, halo_rows, owner_slot, cluster_index,
        coarse_parent.reshape(1, ncd),
    )
    outs = pl.pallas_call(
        functools.partial(finish, float(n * domains) ** (-0.5)),
        out_shape=(
            jax.ShapeDtypeStruct((n, h), BF16),
            jax.ShapeDtypeStruct((n, h), F32),
            big, big, jax.ShapeDtypeStruct((1, h), F32), big, big, big,
        ),
        in_specs=[vmem] * 8,
        out_specs=[vmem] * 8,
        compiler_params=pltpu.CompilerParams(vmem_limit_bytes=60 * 1024 * 1024),
    )(*outs)
    return outs[:4] + (outs[4].reshape(h),) + outs[5:]


def solution(mesh):
    rows = P(("groups", "dom"), None)
    in_specs = (
        rows, rows, P(), P(), P(), P(), P(), P(), rows, rows,
        P(("groups", "dom"), None, None), rows, rows, rows, P(("groups", "dom")),
    )
    mat = P("groups", None)
    out_specs = (rows, rows, mat, mat, P("groups"), mat, mat, mat)
    return jax.shard_map(shards, mesh=mesh, in_specs=in_specs, out_specs=out_specs, check_vma=False)
```

```python
import functools

import jax
import jax.numpy as jnp
from jax import lax
from jax.experimental import pallas as pl
from jax.experimental.pallas import tpu as pltpu
from jax.sharding import PartitionSpec as P

DEG = 8
PW = 8
NCC = 256
OFFSETS = (1, -1, PW, -PW)
F32 = jnp.float32
BF16 = jnp.bfloat16


def mm(left, right):
    return lax.dot_general(left, right, (((1,), (0,)), ((), ())), preferred_element_type=F32)


def tn(left, right):
    return lax.dot_general(left, right, (((0,), (0,)), ((), ())), preferred_element_type=F32)


def nt(left, right):
    return lax.dot_general(left, right, (((1,), (1,)), ((), ())), preferred_element_type=F32)


def halves(values):
    high = values.astype(BF16)
    return high, (values - high.astype(F32)).astype(BF16)


def mm_exact(hot, values):
    high, low = halves(values)
    return mm(hot, high) + mm(hot, low)


def tn_exact(hot, values):
    high, low = halves(values)
    return tn(hot, high) + tn(hot, low)


def gate_of(values):
    return 0.5 * jnp.tanh(0.5 * values) + 0.5


def one_hot(ids, count):
    rows = lax.broadcasted_iota(jnp.int32, (count, ids.shape[1]), 0)
    return jnp.where(rows == ids, 1.0, 0.0).astype(BF16)


def kernel(
    domains, cap, block,
    feat, og, sw, rw, bias, cw, tw, ow, es, er, hr, osl, ci, cp,
    updated, fgrad, wf0, wf1, wf2, bg, cwg, twg,
    hsend, table, hots, sgrad, mt, dj, dpart, dpl, dps, dland, dfull, ph, hid, cpart, cpl, cps, cland, cfull,
    dhal, hret, wp0, wp1, wp2, wq0, wq1, wq2, ws0, ws1, ws2, wl0, wl1, wl2, bmine, bland,
    halo_s, halo_r, ret_s, ret_r, stage_s, stage_r,
):
    me = lax.axis_index("dom")
    n = feat.shape[0]
    slots = hr.shape[2]
    ncd = cp.shape[1]
    h = feat.shape[1]
    wrows = wl0.shape[1]
    wparts, wplands, wpsums = (wp0, wp1, wp2), (wq0, wq1, wq2), (ws0, ws1, ws2)
    wlands, wfulls = (wl0, wl1, wl2), (wf0, wf1, wf2)
    nc = ncd * domains
    edges = es.shape[1]
    blocks = edges // block
    gscale = float(n * domains) ** (-0.5)
    top_scale = (NCC / nc) ** 0.5

    def to_peers(action):
        def body(i, carry):
            action(lax.rem(me + i, domains))
            return carry
        lax.fori_loop(1, domains, body, 0)

    def rdma(src, dst, s, r, peer):
        return pltpu.make_async_remote_copy(
            src_ref=src, dst_ref=dst, send_sem=s, recv_sem=r,
            device_id={"dom": peer}, device_id_type=pl.DeviceIdType.MESH,
        )

    def drain(ref, sem):
        pltpu.make_async_copy(ref, ref, sem).wait()

    half = domains // 2
    slot = lax.div(me, 2)
    par = lax.rem(me, 2)
    partner = me + 1 - 2 * par
    wown = h // wrows // 2

    def piece(start, count):
        return pl.ds(pl.multiple_of(start * count, count), count)

    def if_owner(oh, action):
        if oh == half:
            action()
        else:
            pl.when(slot < oh)(action)

    def same_parity(action):
        def body(i, carry):
            other = lax.rem(slot + i, half)
            action(other, 2 * other + par)
            return carry
        lax.fori_loop(1, half, body, 0)

    def pair_start(part, pland, k):
        rows = pland.shape[0]
        rdma(part.at[piece(1 - par, rows)], pland, stage_s.at[4 * k], stage_r.at[4 * k], partner).start()

    def scatter_start(part, pland, psum, land, k, oh):
        rows, count = pland.shape[0], land.shape[1]
        drain(pland, stage_r.at[4 * k])
        psum[...] = (part[piece(par, rows), :] + pland[...]).astype(BF16)

        def act(other, peer):
            def go():
                rdma(psum.at[piece(other, count)], land.at[slot],
                     stage_s.at[4 * k + 1], stage_r.at[4 * k + 1], peer).start()
            if oh == half:
                go()
            else:
                pl.when(other < oh)(go)
        same_parity(act)

        def own():
            land[slot] = psum[piece(slot, count), :]
        if_owner(oh, own)

    def land_sum(land, k):
        drain(land.at[pl.ds(0, half - 1)], stage_r.at[4 * k + 1])
        return jnp.sum(land[...].astype(F32), axis=0)

    def gather_start(full, values, k, oh):
        count = values.shape[0]
        index = par * oh + slot
        full[piece(index, count), :] = values
        mine = full.at[piece(index, count)]
        same_parity(lambda other, peer: rdma(
            mine, mine, stage_s.at[4 * k + 2], stage_r.at[4 * k + 2], peer).start())

    def block_drain(ref, sem, oh, count):
        if oh == half:
            drain(ref.at[pl.ds(0, (oh - 1) * count)], sem)
        else:
            @pl.when(slot < oh)
            def _():
                drain(ref.at[pl.ds(0, (oh - 1) * count)], sem)

            @pl.when(slot >= oh)
            def _():
                drain(ref.at[pl.ds(0, oh * count)], sem)

    def forward(full, k, oh, count):
        rows = oh * count
        block_drain(full, stage_r.at[4 * k + 2], oh, count)
        mine = full.at[piece(par, rows)]
        rdma(mine, mine, stage_s.at[4 * k + 3], stage_r.at[4 * k + 3], partner).start()

    def full_wait(full, k, oh, count):
        drain(full.at[pl.ds(0, oh * count)], stage_r.at[4 * k + 3])

    def w_gather(m):
        def act():
            gather_start(wfulls[m], land_sum(wlands[m], 2 + m).astype(BF16), 2 + m, wown)
        if_owner(wown, act)

    barrier = pltpu.get_barrier_semaphore()
    to_peers(lambda peer: pl.semaphore_signal(
        barrier, inc=1, device_id={"dom": peer}, device_id_type=pl.DeviceIdType.MESH))

    features = feat[...]
    for k in range(4):
        hsend[k] = tn(one_hot(hr[0, k:k + 1, :], n), features).astype(BF16)
    owner = jnp.floor((osl[...].astype(F32) + 0.5) * (1.0 / cap))
    chip = jnp.floor(owner * 0.5)
    place = (owner - 2.0 * chip) * half + chip
    mt[...] = one_hot(place.astype(jnp.int32) * ncd + ci[...], nc)
    d_joined = nt(og[...], ow[...]).astype(BF16)
    dj[...] = d_joined
    dpart[...] = mm(mt[...], d_joined)
    values = lax.broadcasted_iota(jnp.int32, (NCC, 128), 0).astype(F32).astype(BF16)
    my_parents = tn(one_hot(cp[...], NCC), values).astype(BF16)
    table[0:n, :] = features

    pl.semaphore_wait(barrier, domains - 1)

    def present(offset):
        other = me + offset
        return jnp.logical_and(other >= 0, other < domains)

    def halo_rows_at(ref, k):
        return ref.at[pl.ds(n + k * slots, slots)]

    for k, offset in enumerate(OFFSETS):
        @pl.when(present(offset))
        def _(k=k, offset=offset):
            rdma(hsend.at[k], halo_rows_at(table, k), halo_s.at[k], halo_r.at[k], me + offset).start()

        @pl.when(jnp.logical_not(present(-offset)))
        def _(k=k):
            table[n + k * slots:n + (k + 1) * slots, :] = jnp.zeros((slots, feat.shape[1]), BF16)
    pair_start(dpart, dpl, 0)
    gather_start(ph, my_parents, 5, half)

    own_send = mm(features, sw[...])
    own_recv = mm(features, rw[...]) + bias[...]
    tr = n + 4 * slots
    for b in range(blocks):
        cols = slice(b * block, (b + 1) * block)
        hots[b, 0:tr, :] = one_hot(es[0:1, cols], tr)
        hots[b, tr:tr + n, :] = one_hot(er[0:1, cols], n)

    scatter_start(dpart, dpl, dps, dland, 0, half)
    for k, offset in enumerate(OFFSETS):
        @pl.when(present(-offset))
        def _(k=k):
            drain(halo_rows_at(table, k), halo_r.at[k])
    halo_proj = mm(table[n:tr, :], sw[...])
    proj = jnp.concatenate([own_send, halo_proj, own_recv], axis=0).T.astype(BF16)

    gather_start(dfull, land_sum(dland, 0).astype(BF16), 0, half)
    aggregate = jnp.zeros((n, feat.shape[1]), F32)
    for b in range(blocks):
        pre = mm(proj, hots[b])
        gate = gate_of(pre)
        act = pre * gate
        sgrad[b] = (gate + act * (1.0 - gate)).astype(BF16)
        aggregate = aggregate + nt(hots[b, tr:tr + n, :], act.astype(BF16))
    hidden = (features.astype(F32) + aggregate * (1.0 / DEG)).astype(BF16)
    hid[...] = hidden
    cpart[...] = mm(mt[...], hidden)
    pair_start(cpart, cpl, 1)
    forward(ph, 5, half, ncd)
    forward(dfull, 0, half, ncd)
    scatter_start(cpart, cpl, cps, cland, 1, half)
    gather_start(cfull, 0.25 * land_sum(cland, 1), 1, half)
    full_wait(ph, 5, half, ncd)
    lanes = lax.broadcasted_iota(jnp.int32, (nc, NCC), 1).astype(F32)
    ids = ph[...].astype(F32)
    ids = jnp.concatenate([ids] * (NCC // 128), axis=1)
    parents = jnp.where(lanes == ids, 1.0, 0.0).astype(BF16)
    full_wait(dfull, 0, half, ncd)
    forward(cfull, 1, half, ncd)
    d_out = dfull[...].astype(F32)
    d_top_sum = tn(parents, dfull[...])
    full_wait(cfull, 1, half, ncd)

    coarse = cfull[...]
    coarse_low = coarse.astype(BF16)
    coarse_act = mm(coarse_low, cw[...])
    cgate = gate_of(coarse_act)
    csilu = coarse_act * cgate
    coarse_mid = coarse + csilu
    top_level = tn_exact(parents, coarse_mid) * top_scale
    top_hi, top_lo = halves(top_level)
    w_hi, w_lo = halves(tw[...])
    top_act = mm(top_hi, w_hi) + (mm(top_hi, w_lo) + mm(top_lo, w_hi))
    tgate = gate_of(top_act)
    tsilu = top_act * tgate
    coarse_out = (coarse_mid + mm_exact(parents, tsilu)).astype(BF16)
    joined = (hid[...].astype(F32) + tn(mt[...], coarse_out)).astype(BF16)
    wp0[...] = tn(joined, og[...])
    pair_start(wp0, wq0, 2)
    d_top_act = d_top_sum * (tgate + tsilu * (1.0 - tgate))
    dt_hi, dt_lo = halves(d_top_act)
    d_top = nt(dt_hi, w_hi) + (nt(dt_hi, w_lo) + nt(dt_lo, w_hi))
    d_mid = d_out + top_scale * mm_exact(parents, d_top)
    d_act = (d_mid * (cgate + csilu * (1.0 - cgate))).astype(BF16)
    d_coarse = (d_mid + nt(d_act, cw[...])).astype(BF16)
    scatter_start(wparts[0], wplands[0], wpsums[0], wlands[0], 2 + 0, wown)
    d_hidden = dj[...].astype(F32) + 0.25 * tn(mt[...], d_coarse)
    fgrad[...] = d_hidden
    d_agg = (d_hidden * (1.0 / DEG)).T.astype(BF16)

    d_proj = jnp.zeros((tr + n, feat.shape[1]), F32)
    for b in range(blocks):
        d_pre = mm(d_agg, hots[b, tr:tr + n, :]) * sgrad[b].astype(F32)
        d_proj = d_proj + nt(hots[b], d_pre.astype(BF16))
    d_send = d_proj[0:tr].astype(BF16)
    d_recv_full = d_proj[tr:tr + n]
    d_recv = d_recv_full.astype(BF16)
    bsum = jnp.sum(d_recv_full, axis=0, keepdims=True)
    bmine[...] = bsum
    bland[me] = bmine[...]
    to_peers(lambda peer: rdma(bmine, bland.at[me], stage_s.at[24], stage_r.at[24], peer).start())
    wp1[...] = tn(table[...], d_send)
    pair_start(wp1, wq1, 3)
    wp2[...] = tn(features, d_recv)
    pair_start(wp2, wq2, 4)
    d_table = nt(d_send, sw[...])
    dhal[...] = d_table[n:tr].astype(BF16)
    for k, offset in enumerate(OFFSETS):
        rows = pl.ds(k * slots, slots)

        @pl.when(present(-offset))
        def _(k=k, offset=offset, rows=rows):
            rdma(dhal.at[rows], hret.at[rows], ret_s.at[k], ret_r.at[k], me - offset).start()

        @pl.when(jnp.logical_not(present(offset)))
        def _(k=k):
            hret[k * slots:(k + 1) * slots, :] = jnp.zeros((slots, feat.shape[1]), BF16)

    scatter_start(wparts[1], wplands[1], wpsums[1], wlands[1], 2 + 1, wown)
    scatter_start(wparts[2], wplands[2], wpsums[2], wlands[2], 2 + 2, wown)
    w_gather(0)
    fgrad[...] += d_table[0:n] + nt(d_recv, rw[...])
    updated[...] = mm(joined, ow[...]).astype(BF16)
    twg[...] = gscale * (tn(top_hi, dt_hi) + (tn(top_hi, dt_lo) + tn(top_lo, dt_hi)))
    cwg[...] = gscale * tn(coarse_low, d_act)
    w_gather(1)
    w_gather(2)
    forward(wf0, 2, wown, wrows)
    for k, offset in enumerate(OFFSETS):
        @pl.when(present(offset))
        def _(k=k):
            drain(hret.at[pl.ds(k * slots, slots)], ret_r.at[k])
    back = jnp.zeros((n, feat.shape[1]), F32)
    for k in range(4):
        back = back + mm(one_hot(hr[0, k:k + 1, :], n), hret[k * slots:(k + 1) * slots, :])
    fgrad[...] += back
    drain(bland.at[pl.ds(0, domains - 1)], stage_r.at[24])
    bg[...] = gscale * jnp.sum(bland[...], axis=0)
    forward(wf1, 3, wown, wrows)
    forward(wf2, 4, wown, wrows)
    for m in range(3):
        full_wait(wfulls[m], 2 + m, wown, wrows)

    for k, offset in enumerate(OFFSETS):
        @pl.when(present(offset))
        def _(k=k):
            drain(hsend.at[k], halo_s.at[k])

        @pl.when(present(-offset))
        def _(k=k):
            drain(dhal.at[pl.ds(k * slots, slots)], ret_s.at[k])
    stages = [(dpl, dps, dland, dfull, half, ncd, 0), (cpl, cps, cland, cfull, half, ncd, 1)]
    for m in range(3):
        stages.append((wplands[m], wpsums[m], wlands[m], wfulls[m], wown, wrows, 2 + m))
    for pland, psum, land, full, oh, count, k in stages:
        drain(pland, stage_s.at[4 * k])
        block_drain(psum, stage_s.at[4 * k + 1], oh, count)
    stages.append((None, None, None, ph, half, ncd, 5))
    for pland, psum, land, full, oh, count, k in stages:
        def sent(full=full, land=land, oh=oh, count=count, k=k):
            if oh == half:
                drain(full.at[pl.ds(0, (half - 1) * count)], stage_s.at[4 * k + 2])
            else:
                drain(land.at[pl.ds(0, half - 1)], stage_s.at[4 * k + 2])
        if_owner(oh, sent)
        drain(full.at[pl.ds(0, oh * count)], stage_s.at[4 * k + 3])
    drain(bland.at[pl.ds(0, domains - 1)], stage_s.at[24])


def finish(
    gscale, updated_in, fgrad_in, w0, w1, w2, bias_in, coarse_in, top_in,
    updated, fgrad, swg, rwg, bg, cwg, twg, owg,
):
    updated[...] = updated_in[...]
    fgrad[...] = fgrad_in[...]
    owg[...] = gscale * w0[...].astype(F32)
    swg[...] = gscale * w1[...].astype(F32)
    rwg[...] = gscale * w2[...].astype(F32)
    bg[...] = bias_in[...]
    cwg[...] = coarse_in[...]
    twg[...] = top_in[...]


def shards(
    features, out_grad, send_weight, recv_weight, edge_bias, coarse_weight, top_weight, out_weight,
    edge_sender, edge_receiver, halo_rows, owner_slot, cluster_index, slot_coarse, coarse_parent,
):
    domains = lax.axis_size("dom")
    n, h = features.shape
    ncd = coarse_parent.shape[0]
    nc = ncd * domains
    slots = halo_rows.shape[2]
    tr = n + 4 * slots
    edges = edge_sender.shape[1]
    block = min(edges, 512)
    blocks = edges // block
    cap = slot_coarse.shape[1] // domains
    wrows = max(16, h // domains)
    vmem = pl.BlockSpec(memory_space=pltpu.VMEM)
    dma = pltpu.SemaphoreType.DMA
    scratch = [
        pltpu.VMEM((4, slots, h), BF16),
        pltpu.VMEM((tr, h), BF16),
        pltpu.VMEM((blocks, tr + n, block), BF16),
        pltpu.VMEM((blocks, h, block), BF16),
        pltpu.VMEM((nc, n), BF16),
        pltpu.VMEM((n, h), BF16),
        pltpu.VMEM((nc, h), F32),
        pltpu.VMEM((nc // 2, h), F32),
        pltpu.VMEM((nc // 2, h), BF16),
        pltpu.VMEM((domains // 2, ncd, h), BF16),
        pltpu.VMEM((nc, h), BF16),
        pltpu.VMEM((nc, 128), BF16),
        pltpu.VMEM((n, h), BF16),
        pltpu.VMEM((nc, h), F32),
        pltpu.VMEM((nc // 2, h), F32),
        pltpu.VMEM((nc // 2, h), BF16),
        pltpu.VMEM((domains // 2, ncd, h), BF16),
        pltpu.VMEM((nc, h), F32),
        pltpu.VMEM((4 * slots, h), BF16),
        pltpu.VMEM((4 * slots, h), BF16),
        *[pltpu.VMEM((h, h), F32)] * 3,
        *[pltpu.VMEM((h // 2, h), F32)] * 3,
        *[pltpu.VMEM((h // 2, h), BF16)] * 3,
        *[pltpu.VMEM((domains // 2, wrows, h), BF16)] * 3,
        pltpu.VMEM((1, h), F32),
        pltpu.VMEM((domains, 1, h), F32),
        dma((4,)), dma((4,)), dma((4,)), dma((4,)), dma((25,)), dma((25,)),
    ]
    big = jax.ShapeDtypeStruct((h, h), F32)
    outs = pl.pallas_call(
        functools.partial(kernel, domains, cap, block),
        out_shape=(
            jax.ShapeDtypeStruct((n, h), BF16),
            jax.ShapeDtypeStruct((n, h), F32),
            *[jax.ShapeDtypeStruct((h, h), BF16)] * 3, jax.ShapeDtypeStruct((1, h), F32), big, big,
        ),
        in_specs=[vmem] * 14,
        out_specs=[vmem] * 8,
        scratch_shapes=scratch,
        compiler_params=pltpu.CompilerParams(
            collective_id=0, has_side_effects=True, vmem_limit_bytes=56 * 1024 * 1024
        ),
    )(
        features, out_grad, send_weight, recv_weight, edge_bias.reshape(1, h), coarse_weight,
        top_weight, out_weight, edge_sender, edge_receiver, halo_rows, owner_slot, cluster_index,
        coarse_parent.reshape(1, ncd),
    )
    outs = pl.pallas_call(
        functools.partial(finish, float(n * domains) ** (-0.5)),
        out_shape=(
            jax.ShapeDtypeStruct((n, h), BF16),
            jax.ShapeDtypeStruct((n, h), F32),
            big, big, jax.ShapeDtypeStruct((1, h), F32), big, big, big,
        ),
        in_specs=[vmem] * 8,
        out_specs=[vmem] * 8,
        compiler_params=pltpu.CompilerParams(vmem_limit_bytes=60 * 1024 * 1024),
    )(*outs)
    return outs[:4] + (outs[4].reshape(h),) + outs[5:]


def solution(mesh):
    rows = P(("groups", "dom"), None)
    in_specs = (
        rows, rows, P(), P(), P(), P(), P(), P(), rows, rows,
        P(("groups", "dom"), None, None), rows, rows, rows, P(("groups", "dom")),
    )
    mat = P("groups", None)
    out_specs = (rows, rows, mat, mat, P("groups"), mat, mat, mat)
    return jax.shard_map(shards, mesh=mesh, in_specs=in_specs, out_specs=out_specs, check_vma=False)
```
